32 devices in a mesh: groups: 2 (over x), expert: 16 (over z, y, core).
Axes of the slice: x: 2, y: 2, z: 4, core: 2. Of those that a mesh axis runs over, the one named last changes fastest.
Arguments:
- residual: bfloat16 [64, 7168], P(('groups', 'expert')), parts along dimension 0, may hold values from -6 to 6
- attention: bfloat16 [64, 2048], P('groups', 'expert'), parts along dimension 0, may hold values from -6 to 6
- out_weight: bfloat16 [2048, 7168], P('expert'), may hold values from -0.125 to 0.125
- norm_gain: float32 [7168], replicated, may hold values from 0.1 to 1.9
- route_ids: int32 [64, 2], P(('groups', 'expert')), parts along dimension 0, may hold values from 0 to 3, all different within a row; in each aligned block of 2 rows (0 to 1, 2 to 3, ...) at most 2 rows name the same one
- route_weight: float32 [64, 2], P(('groups', 'expert')), parts along dimension 0, may hold values from 0.2 to 1
- gate_weight: bfloat16 [16, 7168, 256], P('expert'), may hold values from -0.0625 to 0.0625
- up_weight: bfloat16 [16, 7168, 256], P('expert'), may hold values from -0.0625 to 0.0625
- down_weight: bfloat16 [16, 256, 7168], P('expert'), may hold values from -0.1875 to 0.1875
Outputs:
- mixed: bfloat16 [64, 7168], P(('groups', 'expert')), parts along dimension 0
The draws below stay inside these ranges and needn't reach their ends.
There are 2 independent parts, one for each index of `groups`. The reference program is written for one: setup_inputs(seed, part) draws one part's arguments, and reference() takes and returns one part's arrays. A program takes and returns all parts, laid end to end along the dimension named above; an argument that names none is the same for every part. Nothing has to cross between parts.
Inputs may be any that keep to these rules, and one draw needn't show every extreme that they name: `route_ids`: each row names 2 different experts. In each aligned block of 2 rows (the rows of one device) no expert is named by more than 2 rows, and in some block one expert is named by exactly 2 rows.
All inputs are finite; a program needn't handle non-finite values.
Results may differ from the reference program's by a relative error of at most 0.0038.
Values may be sent and summed in bfloat16 or wider, within the bound.
A program may use at most 64 MiB of HBM per device.

```python
import math
import jax
import jax.numpy as jnp
import numpy as np
from jax import lax

D = 7168
VH = 128
FF_WIN = 1024
TOP = 2
TOK_DEV = 2
SPLIT = 4
FF_DEV = 256
EXPERTS = 4
HEADS = 16
TOKENS = 32
CAP = 2
N_EXPERT = 16


def strengthened(values, rng, source, target, parts, factor):
    owner, partner = [(jnp.arange(values.shape[axis_at]) // (values.shape[axis_at] // parts)).reshape([-1 if axis == axis_at else 1 for axis in range(values.ndim)]) for axis_at in (source, target)]
    chosen = jax.random.permutation(rng, parts)[partner]
    strong = (owner == chosen) | (owner == (partner + parts // 2) % parts)
    return jnp.where(strong, factor * values, values)


def shard_levels(rng, dims, split, least, top_value):
    factor_of, own = 1.0, jax.random.fold_in(rng, 6)
    for axis_at, parts in split:
        draws = jnp.exp(jax.random.uniform(jax.random.fold_in(own, axis_at), (parts,), jnp.float32, least / len(split), top_value / len(split)))
        factor_of = factor_of * jnp.repeat(draws, dims[axis_at] // parts).reshape([-1 if axis == axis_at else 1 for axis in range(len(dims))])
    return factor_of


def assign_block(stream_key, own, number, rows, number_of, top, limit, slope):
    ranking = jax.random.permutation(stream_key, number_of)
    packed, usual = shares(number_of, rows * top, limit, slope, True), shares(number_of, rows * top, limit, slope, False)
    places = jnp.arange(number_of)

    def named(lengths, offset_by):
        used = int((lengths > 0).sum())
        fixed = max(1, used // 4)
        shifted = fixed + (places - fixed + offset_by * (used - fixed)) % max(1, number_of - fixed)
        return jnp.zeros((number_of,), jnp.int32).at[ranking[jnp.where(places < fixed, places, shifted)]].set(jnp.asarray(lengths, jnp.int32))

    lengths = jnp.where(number % 4 == 0, named(packed, number // 4), named(usual, number - number // 4 - 1))
    mixed = jax.random.permutation(jax.random.fold_in(own, 3), number_of)
    giver, sink = mixed[0:number_of // 2 * 2:2], mixed[1:number_of // 2 * 2:2]
    margin = jnp.minimum(lengths[giver] - 1, limit - lengths[sink]) // 2
    margin = jnp.where((giver == ranking[0]) | (sink == ranking[0]) | (lengths[sink] == 0), 0, jnp.maximum(margin, 0))
    shifted = jax.random.randint(jax.random.fold_in(own, 4), (number_of // 2,), 0, 1 << 20) % (margin + 1)
    lengths = lengths.at[giver].add(-shifted).at[sink].add(shifted)
    items = jnp.searchsorted(jnp.cumsum(lengths), jnp.arange(rows * top), side="right").astype(jnp.int32)
    listing = items.reshape(top, rows).T
    listing = listing[jax.random.permutation(jax.random.fold_in(own, 1), rows)]
    offset_by = jax.random.randint(jax.random.fold_in(own, 2), (rows, 1), 0, top)
    return jnp.take_along_axis(listing, (jnp.arange(top)[None, :] + offset_by) % top, axis=1)


def shares(amount, total, bound, lean, full):
    loads = [(1 << 20) // math.isqrt(grade ** lean) + 1 for grade in range(1, amount + 1)]
    largest = bound if full else min(bound, max(-(-total // amount), total * loads[0] // sum(loads)))
    least = 1 if total - largest >= amount - 1 else 0
    holding, surplus = [largest] + [least] * (amount - 1), total - largest - least * (amount - 1)
    while surplus > 0:
        movable = [i for i in range(1, amount) if holding[i] < largest] or [i for i in range(1, amount) if holding[i] < bound]
        mass, budget = sum([loads[i] for i in movable]), surplus
        for i in movable:
            extra = min(bound - holding[i], max(1, budget * loads[i] // mass), surplus)
            holding[i] = holding[i] + extra
            surplus = surplus - extra
    return np.array(holding)


def centred(own_key, extent, spread, reach, cuts=(), kind=jnp.bfloat16):
    drawn = spread * jax.random.normal(own_key, extent, jnp.float32)
    if cuts:
        drawn = drawn * shard_levels(own_key, extent, cuts, -0.22, 0.18)
    return jnp.clip(drawn, -reach, reach).astype(kind)


def noise_with(rng, extent, width, most, cuts, heavy, kind=jnp.bfloat16):
    drawn = width * jax.random.normal(rng, extent, jnp.float32)
    if cuts:
        drawn = drawn * shard_levels(rng, extent, cuts, -0.22, 0.18)
    return jnp.clip(strengthened(drawn, jax.random.fold_in(rng, 3), *heavy), -most, most).astype(kind)


def setup_inputs(seed: int = 0, part: int = 0) -> dict:
    streams_of = jax.random.split(jax.random.key(seed), 10)
    own_keys = jax.random.split(jax.random.fold_in(streams_of[9], part), 10)
    residual = centred(own_keys[0], (TOKENS, D), 1.0, 6.0, ((0, 16),))
    attention = noise_with(own_keys[1], (TOKENS, HEADS * VH), 1.0, 6.0, ((1, 16),), (1, 0, 16, 2.0))
    out_weight = centred(streams_of[2], (HEADS * VH, D), (HEADS * VH) ** -0.5, 0.125, ((0, 16),))
    norm_gain = jnp.clip(1.0 + 0.18 * jax.random.normal(streams_of[3], (D,), jnp.float32), 0.1, 1.9)
    route_ids_keys = jax.random.split(jax.random.fold_in(own_keys[4], 1), TOKENS // TOK_DEV)
    route_ids_turns = jax.random.permutation(jax.random.fold_in(own_keys[4], 3), TOKENS // TOK_DEV)
    route_ids = jax.vmap(lambda own, number: assign_block(jax.random.fold_in(own_keys[4], 2), own, number, TOK_DEV, EXPERTS, TOP, CAP, 2))(route_ids_keys, route_ids_turns).reshape((TOKENS, TOP))
    route_weight = jnp.clip(0.2 + 0.8 * jax.random.uniform(own_keys[5], (TOKENS, TOP), jnp.float32) ** shard_levels(own_keys[5], (TOKENS, TOP), ((0, 16),), -0.2, 0.2), 0.2, 1.0)
    gate_weight = centred(streams_of[6], (EXPERTS * SPLIT, D, FF_DEV), D ** -0.5, 0.0625, ((0, 16),))
    up_weight = centred(streams_of[7], (EXPERTS * SPLIT, D, FF_DEV), D ** -0.5, 0.0625, ((0, 16),))
    down_weight = centred(streams_of[8], (EXPERTS * SPLIT, FF_DEV, D), FF_WIN ** -0.5, 0.1875, ((0, 16),))
    return dict(residual=residual, attention=attention, out_weight=out_weight, norm_gain=norm_gain, route_ids=route_ids, route_weight=route_weight, gate_weight=gate_weight, up_weight=up_weight, down_weight=down_weight)


EPSILON = 1e-06

def reference(residual, attention, out_weight, norm_gain, route_ids, route_weight, gate_weight, up_weight, down_weight):
    hidden_state = residual.astype(jnp.float32) + jnp.dot(attention, out_weight, preferred_element_type=jnp.float32)
    inv_rms = lax.rsqrt(lax.optimization_barrier(jnp.mean(hidden_state * hidden_state, axis=-1, keepdims=True)) + EPSILON)
    normed = (hidden_state * inv_rms * norm_gain).astype(jnp.bfloat16)
    gate_stack = gate_weight.reshape(EXPERTS, SPLIT, D, FF_DEV)
    up_stack = up_weight.reshape(EXPERTS, SPLIT, D, FF_DEV)
    down_stack = down_weight.reshape(EXPERTS, SPLIT, FF_DEV, D)
    row_limit = N_EXPERT * CAP

    def add_expert(summed, expert):
        gate_full = gate_stack[expert].transpose(1, 0, 2).reshape(D, SPLIT * FF_DEV)
        up_full = up_stack[expert].transpose(1, 0, 2).reshape(D, SPLIT * FF_DEV)
        routed = route_ids == expert
        route_coef = lax.optimization_barrier(jnp.sum(jnp.where(routed, route_weight, jnp.zeros_like(route_weight)), axis=1))
        touched = jnp.any(routed, axis=1)
        hit_count = jnp.sum(touched.astype(jnp.int32))
        row_ids = jnp.nonzero(touched, size=row_limit, fill_value=0)[0].astype(jnp.int32)
        is_live = jnp.arange(row_limit, dtype=jnp.int32) < hit_count
        picked = normed[row_ids]
        gate_out = jnp.dot(picked, gate_full, preferred_element_type=jnp.float32)
        up_out = jnp.dot(picked, up_full, preferred_element_type=jnp.float32)
        activated = (jax.nn.silu(gate_out) * up_out).astype(jnp.bfloat16)
        pieces = jnp.einsum('rsf,sfd->rsd', activated.reshape(row_limit, SPLIT, FF_DEV).astype(jnp.float32), down_stack[expert].astype(jnp.float32))
        pieces = lax.optimization_barrier(pieces.astype(jnp.bfloat16)).astype(jnp.float32)
        expert_out = lax.optimization_barrier(jnp.sum(pieces, axis=1))
        row_weight = jnp.where(is_live, route_coef[row_ids], jnp.zeros_like(route_coef[row_ids]))
        summed = summed.at[row_ids].add(row_weight[:, None] * expert_out)
        return (summed, None)
    summed = lax.scan(add_expert, jnp.zeros((TOKENS, D), jnp.float32), jnp.arange(EXPERTS, dtype=jnp.int32))[0]
    return (hidden_state + summed).astype(jnp.bfloat16)
```

```python
import functools

import jax
import jax.numpy as jnp
from jax import lax
from jax.experimental import pallas as pl
from jax.experimental.pallas import tpu as pltpu
from jax.sharding import PartitionSpec as P

FF_WIN = 1024
EPSILON = 1e-06
PIECES = 8
META = 128
CHUNKS = ((0, 512), (512, 384))
MESH = pl.DeviceIdType.MESH


def split_three(value):
    high = value.astype(jnp.bfloat16).astype(jnp.float32)
    rest = value - high
    middle = rest.astype(jnp.bfloat16).astype(jnp.float32)
    return high, middle, rest - middle


def kernel(
    n,
    expert_split,
    residual,
    attention,
    gain,
    route_ids,
    route_weight,
    wo_hbm,
    wg_hbm,
    wu_hbm,
    wd_hbm,
    out,
    wo,
    wg,
    wu,
    wd,
    partial,
    gathered,
    tokens,
    hidden,
    gain_tile,
    meta,
    send_c,
    recv_c,
    send_b,
    recv_b,
    send_a,
    recv_a,
    load_sem,
    c_sem,
    b_sem,
    a_sem,
    gc_sem,
    gb_sem,
    ga_sem,
):
    width = gain_tile.shape[1]
    far = n // 4
    top = route_ids.shape[1]
    steps = range(len(CHUNKS))
    last = len(CHUNKS) - 1
    me = lax.axis_index("expert")
    a, b, c = me // 4, (me // 2) % 2, me % 2
    peer_c, peer_b = me + 1 - 2 * c, me + 2 - 4 * b
    peers_a = [lax.rem(me + 4 * d, n) for d in range(1, far)]

    loads = [
        pltpu.make_async_copy(wo_hbm, wo, load_sem.at[0]),
        pltpu.make_async_copy(wg_hbm.at[0], wg, load_sem.at[1]),
        pltpu.make_async_copy(wu_hbm.at[0], wu, load_sem.at[2]),
        pltpu.make_async_copy(wd_hbm.at[0], wd, load_sem.at[3]),
    ]
    for load in loads:
        load.start()

    barrier = pltpu.get_barrier_semaphore()
    for peer in [peer_c, peer_b] + peers_a:
        pl.semaphore_signal(barrier, inc=1, device_id={"expert": peer}, device_id_type=MESH)

    def remote(src, dst, sems, peer):
        return pltpu.make_async_remote_copy(
            src_ref=src,
            dst_ref=dst,
            send_sem=sems.at[0],
            recv_sem=sems.at[1],
            device_id={"expert": peer},
            device_id_type=MESH,
        )

    def lanes(k):
        return pl.ds(*CHUNKS[k])

    def wide(k):
        start, size = CHUNKS[k]
        return pl.ds(start, size + (META if k == last else 0))

    copies_c = [
        [
            remote(send_c.at[r, :, :, lanes(k)], recv_c.at[r, :, :, lanes(k)], c_sem.at[r, k], peer_c)
            for k in steps
        ]
        for r in range(2)
    ]
    copies_b = [
        [
            remote(send_b.at[r, :, :, lanes(k)], recv_b.at[r, :, :, lanes(k)], b_sem.at[r, k], peer_b)
            for k in steps
        ]
        for r in range(2)
    ]
    copies_a = [
        [
            [
                remote(
                    send_a.at[r, d, :, lanes(k)],
                    recv_a.at[r, d, :, lanes(k)],
                    a_sem.at[r, k, d],
                    peers_a[d],
                )
                for d in range(far - 1)
            ]
            for k in steps
        ]
        for r in range(2)
    ]
    gathers_a = [
        [
            remote(
                gathered.at[a, b, c, :, wide(k)],
                gathered.at[a, b, c, :, wide(k)],
                ga_sem.at[k, d],
                peers_a[d],
            )
            for d in range(far - 1)
        ]
        for k in steps
    ]
    gathers_b = [
        remote(gathered.at[:, b, c, :, wide(k)], gathered.at[:, b, c, :, wide(k)], gb_sem.at[k], peer_b)
        for k in steps
    ]
    gathers_c = [
        remote(gathered.at[:, :, c, :, wide(k)], gathered.at[:, :, c, :, wide(k)], gc_sem.at[k], peer_c)
        for k in steps
    ]

    def block(owner, k):
        start, size = CHUNKS[k]
        return partial[pl.ds(2 * owner, 2), :, start : start + size].reshape(2 * PIECES, size)

    def keep(owner, k, value):
        start, size = CHUNKS[k]
        partial[pl.ds(2 * owner, 2), :, start : start + size] = value.reshape(2, PIECES, size)

    def spread(k, left, right, scale):
        start, size = CHUNKS[k]
        for j in range(PIECES):
            at = j * width + start
            product = jnp.dot(left, right[:, at : at + size], preferred_element_type=jnp.float32)
            partial[:, j, start : start + size] = product if scale is None else product * scale

    def first(r, k):
        start, size = CHUNKS[k]

        @pl.loop(0, 2 * far)
        def _(i):
            value = block(2 * i + 1 - c, k).astype(jnp.bfloat16)
            send_c[r, i, :, start : start + size] = value

    def second(r, k):
        start, size = CHUNKS[k]
        copies_c[r][k].wait_recv()

        def total(i):
            received = recv_c[r, i, :, start : start + size].astype(jnp.float32)
            return block(2 * i + c, k) + received

        @pl.loop(0, far)
        def _(q):
            send_b[r, q, :, start : start + size] = total(2 * q + 1 - b).astype(jnp.bfloat16)

        copies_b[r][k].start()

        @pl.loop(0, far)
        def _(q):
            i = 2 * q + b
            keep(2 * i + c, k, total(i))

    def third(r, k):
        start, size = CHUNKS[k]
        copies_b[r][k].wait_recv()

        def total(q):
            received = recv_b[r, q, :, start : start + size].astype(jnp.float32)
            return block(4 * q + 2 * b + c, k) + received

        for d in range(far - 1):
            value = total(peers_a[d] // 4).astype(jnp.bfloat16)
            send_a[r, d, :, start : start + size] = value
            copies_a[r][k][d].start()
        keep(me, k, total(a))

    def fourth(r, k):
        start, size = CHUNKS[k]
        value = block(me, k)
        for d in range(far - 1):
            copies_a[r][k][d].wait_recv()
            value = value + recv_a[r, d, :, start : start + size].astype(jnp.float32)
        return value.reshape(2, PIECES, size)

    lane = lax.broadcasted_iota(jnp.int32, (1, META), 1)
    meta[...] = jnp.zeros_like(meta)
    for row in range(2):
        coef = jnp.zeros((1, META), jnp.float32)
        for k in range(top):
            chosen = route_ids[row : row + 1, k : k + 1] == lane
            coef = coef + jnp.where(chosen, route_weight[row : row + 1, k : k + 1], 0.0)
        for place, value in enumerate(split_three(coef)):
            meta[row, 3 + place : 4 + place, :] = value
    for j in range(PIECES):
        hidden[:, j, :] = residual[:, j * width : (j + 1) * width].astype(jnp.float32)
        gain_tile[j : j + 1, :] = gain[:, j * width : (j + 1) * width]

    squares = []

    def normed(k):
        start, size = CHUNKS[k]
        value = hidden[:, :, start : start + size] + fourth(0, k)
        hidden[:, :, start : start + size] = value
        scaled = value * gain_tile[:, start : start + size][None]
        gathered[a, b, c, :, start : start + size] = scaled.reshape(2 * PIECES, size).astype(
            jnp.bfloat16
        )
        part = jnp.sum(jnp.sum(value * value, axis=2, keepdims=True), axis=1, keepdims=True)
        squares.append(part)
        if k == last:
            total = sum(squares[1:], squares[0])
            for row in range(2):
                spreaded = jnp.broadcast_to(total[row], (1, META))
                for place, piece in enumerate(split_three(spreaded)):
                    meta[row, place : place + 1, :] = piece
            gathered[a, b, c, :, width:] = meta[...].reshape(2 * PIECES, META).astype(jnp.bfloat16)
        for copy in gathers_a[k]:
            copy.start()

    def pass_b(k):
        for copy in gathers_a[k]:
            copy.wait_recv()
        gathers_b[k].start()

    def pass_c(k):
        gathers_b[k].wait_recv()
        gathers_c[k].start()

    products = []

    def consume(k):
        start, size = CHUNKS[k]
        size_wide = size + (META if k == last else 0)
        gathers_c[k].wait_recv()

        @pl.loop(0, n)
        def _(owner):
            value = gathered[owner // 4, (owner // 2) % 2, owner % 2, :, start : start + size_wide]
            tokens[pl.ds(2 * owner, 2), :, start : start + size_wide] = value.astype(
                jnp.float32
            ).reshape(2, PIECES, size_wide)

        if k == 0:
            loads[1].wait()
            loads[2].wait()
        for j in range(PIECES):
            rows = tokens[:, j, start : start + size].astype(jnp.bfloat16)
            at = j * width + start
            products.append(
                (
                    jnp.dot(rows, wg[at : at + size, :], preferred_element_type=jnp.float32),
                    jnp.dot(rows, wu[at : at + size, :], preferred_element_type=jnp.float32),
                )
            )
            if len(products) > 1:
                later, earlier = products.pop(), products.pop()
                products.append((earlier[0] + later[0], earlier[1] + later[1]))

    def project(k):
        if k == 0:
            loads[0].wait()
        spread(k, attention[...], wo, None)
        first(0, k)
        if k == 0:
            pl.semaphore_wait(barrier, far + 1)
        copies_c[0][k].start()

    stages = [
        project,
        lambda k: second(0, k),
        lambda k: third(0, k),
        normed,
        pass_b,
        pass_c,
        consume,
    ]
    for step in range(len(stages) + last):
        for k in steps:
            if 0 <= step - k < len(stages):
                stages[step - k](k)

    gate, up = products[0]
    mean = (tokens[:, 0, width:] + tokens[:, 1, width:] + tokens[:, 2, width:]) * (
        1.0 / (PIECES * width)
    )
    inv_rms = lax.rsqrt(mean + EPSILON)[:, :1]
    coefs = tokens[:, 3, width:] + tokens[:, 4, width:] + tokens[:, 5, width:]
    coef = jnp.sum(jnp.where(lane == me // expert_split, coefs, 0.0), axis=1, keepdims=True)
    gate, up = gate * inv_rms, up * inv_rms
    act = (gate / (1.0 + jnp.exp(-gate)) * up).astype(jnp.bfloat16)
    loads[3].wait()

    def down(k):
        spread(k, act, wd, coef)
        first(1, k)
        copies_c[1][k].start()

    def final(k):
        start, size = CHUNKS[k]
        hidden[:, :, start : start + size] = hidden[:, :, start : start + size] + fourth(1, k)
        for j in range(PIECES):
            at = j * width + start
            out[:, at : at + size] = hidden[:, j, start : start + size].astype(out.dtype)

    stages = [down, lambda k: second(1, k), lambda k: third(1, k), final]
    for step in range(len(stages) + last):
        for k in steps:
            if 0 <= step - k < len(stages):
                stages[step - k](k)

    for k in steps:
        for r in range(2):
            for copy in [copies_c[r][k], copies_b[r][k]] + copies_a[r][k]:
                copy.wait_send()
        for copy in gathers_a[k] + [gathers_b[k], gathers_c[k]]:
            copy.wait_send()


def local(
    residual,
    attention,
    out_weight,
    norm_gain,
    route_ids,
    route_weight,
    gate_weight,
    up_weight,
    down_weight,
):
    n = lax.axis_size("expert")
    rows, model = residual.shape
    width = model // PIECES
    hidden_units = gate_weight.shape[2]
    far = n // 4
    count = len(CHUNKS)
    bf16, f32 = jnp.bfloat16, jnp.float32
    vmem = pl.BlockSpec(memory_space=pltpu.VMEM)
    hbm = pl.BlockSpec(memory_space=pltpu.HBM)
    dma = pltpu.SemaphoreType.DMA
    return pl.pallas_call(
        functools.partial(kernel, n, FF_WIN // hidden_units),
        out_shape=jax.ShapeDtypeStruct((rows, model), bf16),
        in_specs=[vmem] * 5 + [hbm] * 4,
        out_specs=vmem,
        scratch_shapes=[
            pltpu.VMEM(out_weight.shape, bf16),
            pltpu.VMEM(gate_weight.shape[1:], bf16),
            pltpu.VMEM(up_weight.shape[1:], bf16),
            pltpu.VMEM(down_weight.shape[1:], bf16),
            pltpu.VMEM((2 * n, PIECES, width), f32),
            pltpu.VMEM((far, 2, 2, 2 * PIECES, width + META), bf16),
            pltpu.VMEM((2 * n, PIECES, width + META), f32),
            pltpu.VMEM((2, PIECES, width), f32),
            pltpu.VMEM((PIECES, width), f32),
            pltpu.VMEM((2, PIECES, META), f32),
            pltpu.VMEM((2, 2 * far, 2 * PIECES, width), bf16),
            pltpu.VMEM((2, 2 * far, 2 * PIECES, width), bf16),
            pltpu.VMEM((2, far, 2 * PIECES, width), bf16),
            pltpu.VMEM((2, far, 2 * PIECES, width), bf16),
            pltpu.VMEM((2, far - 1, 2 * PIECES, width), bf16),
            pltpu.VMEM((2, far - 1, 2 * PIECES, width), bf16),
            dma((4,)),
            dma((2, count, 2)),
            dma((2, count, 2)),
            dma((2, count, far - 1, 2)),
            dma((count, 2)),
            dma((count, 2)),
            dma((count, far - 1, 2)),
        ],
        compiler_params=pltpu.CompilerParams(
            collective_id=0, has_side_effects=True, vmem_limit_bytes=48 * 1024 * 1024
        ),
    )(
        residual,
        attention,
        norm_gain.reshape(1, model),
        route_ids,
        route_weight,
        out_weight,
        gate_weight,
        up_weight,
        down_weight,
    )


def solution(mesh):
    return jax.shard_map(
        local,
        mesh=mesh,
        in_specs=(
            P(("groups", "expert"), None),
            P("groups", "expert"),
            P("expert", None),
            P(),
            P(("groups", "expert"), None),
            P(("groups", "expert"), None),
            P("expert", None, None),
            P("expert", None, None),
            P("expert", None, None),
        ),
        out_specs=P(("groups", "expert"), None),
        check_vma=False,
    )
```

```python
import functools

import jax
import jax.numpy as jnp
from jax import lax
from jax.experimental import pallas as pl
from jax.experimental.pallas import tpu as pltpu
from jax.sharding import PartitionSpec as P

FF_WIN = 1024
EPSILON = 1e-06
PIECES = 8
META = 128
CHUNKS = ((0, 896),)
MESH = pl.DeviceIdType.MESH


def split_three(value):
    high = value.astype(jnp.bfloat16).astype(jnp.float32)
    rest = value - high
    middle = rest.astype(jnp.bfloat16).astype(jnp.float32)
    return high, middle, rest - middle


def kernel(
    n,
    expert_split,
    residual_hbm,
    attention_hbm,
    gain_hbm,
    ids_hbm,
    weight_hbm,
    wo_hbm,
    wg_hbm,
    wu_hbm,
    wd_hbm,
    out,
    residual,
    attention,
    gain,
    route_ids,
    route_weight,
    wo,
    wg,
    wu,
    wd,
    partial,
    gathered,
    tokens,
    hidden,
    gain_tile,
    meta,
    recv_c,
    send_b,
    recv_b,
    send_a,
    recv_a,
    load_sem,
    c_sem,
    b_sem,
    a_sem,
    gc_sem,
    gb_sem,
    ga_sem,
):
    width = gain_tile.shape[1]
    far = n // 4
    top = route_ids.shape[1]
    steps = range(len(CHUNKS))
    last = len(CHUNKS) - 1
    me = lax.axis_index("expert")
    a, b, c = me // 4, (me // 2) % 2, me % 2
    peer_c, peer_b = me + 1 - 2 * c, me + 2 - 4 * b
    peers_a = [lax.rem(me + 4 * d, n) for d in range(1, far)]

    small = [
        pltpu.make_async_copy(source, target, load_sem.at[4 + place])
        for place, (source, target) in enumerate(
            [
                (attention_hbm, attention),
                (residual_hbm, residual),
                (gain_hbm, gain),
                (ids_hbm, route_ids),
                (weight_hbm, route_weight),
            ]
        )
    ]
    for load in small:
        load.start()
    loads = [
        pltpu.make_async_copy(wo_hbm, wo, load_sem.at[0]),
        pltpu.make_async_copy(wg_hbm.at[0], wg, load_sem.at[1]),
        pltpu.make_async_copy(wu_hbm.at[0], wu, load_sem.at[2]),
        pltpu.make_async_copy(wd_hbm.at[0], wd, load_sem.at[3]),
    ]
    loads[0].start()

    barrier = pltpu.get_barrier_semaphore()
    for peer in [peer_c, peer_b] + peers_a:
        pl.semaphore_signal(barrier, inc=1, device_id={"expert": peer}, device_id_type=MESH)

    def remote(src, dst, sems, peer):
        return pltpu.make_async_remote_copy(
            src_ref=src,
            dst_ref=dst,
            send_sem=sems.at[0],
            recv_sem=sems.at[1],
            device_id={"expert": peer},
            device_id_type=MESH,
        )

    half, quarter = n, n // 2
    other_half, own_half = pl.ds((1 - c) * half, half), c * half
    copies_c, copies_b, copies_a = [], [], []
    for r in range(2):
        copies_c.append([])
        copies_b.append([])
        copies_a.append([])
        for k in steps:
            copies_c[r].append(
                remote(partial[r][k].at[other_half], recv_c[r][k], c_sem.at[r, k], peer_c)
            )
            copies_b[r].append(remote(send_b[r][k], recv_b[r][k], b_sem.at[r, k], peer_b))
            copies_a[r].append(
                [
                    remote(send_a[r][k].at[d], recv_a[r][k].at[d], a_sem.at[r, k, d], peers_a[d])
                    for d in range(far - 1)
                ]
            )
    gathers_a, gathers_b, gathers_c = [], [], []
    for k in steps:
        own, row, plane = gathered[k].at[c, b, a], gathered[k].at[c, b], gathered[k].at[c]
        gathers_a.append([remote(own, own, ga_sem.at[k, d], peers_a[d]) for d in range(far - 1)])
        gathers_b.append(remote(row, row, gb_sem.at[k], peer_b))
        gathers_c.append(remote(plane, plane, gc_sem.at[k], peer_c))

    def spread(r, k, left, right, scale):
        start, size = CHUNKS[k]
        for j in range(PIECES):
            at = j * width + start
            product = jnp.dot(left, right[:, at : at + size], preferred_element_type=jnp.float32)
            partial[r][k][:, j, :] = product if scale is None else product * scale

    def second(r, k):
        size = CHUNKS[k][1]
        copies_c[r][k].wait_recv()
        at = (1 - b) * quarter
        total = partial[r][k][pl.ds(own_half + at, quarter)] + recv_c[r][k][pl.ds(at, quarter)]
        send_b[r][k][...] = total.reshape(far, 2 * PIECES, size).astype(jnp.bfloat16)
        copies_b[r][k].start()

    def third(r, k):
        size = CHUNKS[k][1]
        copies_b[r][k].wait_recv()
        for d in range(far - 1):
            q = peers_a[d] // 4
            at = b * quarter + 2 * q
            total = partial[r][k][pl.ds(own_half + at, 2)] + recv_c[r][k][pl.ds(at, 2)]
            total = total.reshape(2 * PIECES, size) + recv_b[r][k][q].astype(jnp.float32)
            send_a[r][k][d] = total.astype(jnp.bfloat16)
            copies_a[r][k][d].start()

    def fourth(r, k):
        size = CHUNKS[k][1]
        at = b * quarter + 2 * a
        total = partial[r][k][pl.ds(own_half + at, 2)] + recv_c[r][k][pl.ds(at, 2)]
        total = total.reshape(2 * PIECES, size) + recv_b[r][k][a].astype(jnp.float32)
        for d in range(far - 1):
            copies_a[r][k][d].wait_recv()
            total = total + recv_a[r][k][d].astype(jnp.float32)
        return total.reshape(2, PIECES, size)

    for load in small:
        load.wait()
    place = lax.broadcasted_iota(jnp.int32, (2 * n, 2 * n), 0)
    token = lax.broadcasted_iota(jnp.int32, (2 * n, 2 * n), 1)
    bits = quarter.bit_length() - 1
    source = ((place & (quarter - 1)) >> 1) * 8 + ((place >> bits) & 1) * 4
    source = source + (place >> (bits + 1)) * 2 + (place & 1)
    order = jnp.where(source == token, 1.0, 0.0).astype(jnp.bfloat16)
    heads = jnp.dot(order, attention[...], preferred_element_type=jnp.float32).astype(jnp.bfloat16)
    lane = lax.broadcasted_iota(jnp.int32, (1, META), 1)
    meta[...] = jnp.zeros_like(meta)
    for row in range(2):
        coef = jnp.zeros((1, META), jnp.float32)
        for k in range(top):
            chosen = route_ids[row : row + 1, k : k + 1] == lane
            coef = coef + jnp.where(chosen, route_weight[row : row + 1, k : k + 1], 0.0)
        for place, value in enumerate(split_three(coef)):
            meta[row, 3 + place : 4 + place, :] = value
    for j in range(PIECES):
        hidden[:, j, :] = residual[:, j * width : (j + 1) * width].astype(jnp.float32)
        gain_tile[j : j + 1, :] = gain[:, j * width : (j + 1) * width]

    squares = []

    def normed(k):
        start, size = CHUNKS[k]
        value = hidden[:, :, start : start + size] + fourth(0, k)
        hidden[:, :, start : start + size] = value
        scaled = value * gain_tile[:, start : start + size][None]
        gathered[k][c, b, a, :, :size] = scaled.reshape(2 * PIECES, size).astype(jnp.bfloat16)
        part = jnp.sum(jnp.sum(value * value, axis=2, keepdims=True), axis=1, keepdims=True)
        squares.append(part)
        if k == last:
            total = sum(squares[1:], squares[0])
            for row in range(2):
                spreaded = jnp.broadcast_to(total[row], (1, META))
                for place, piece in enumerate(split_three(spreaded)):
                    meta[row, place : place + 1, :] = piece
            gathered[k][c, b, a, :, size:] = meta[...].reshape(2 * PIECES, META).astype(jnp.bfloat16)
        for copy in gathers_a[k]:
            copy.start()

    def pass_b(k):
        for copy in gathers_a[k]:
            copy.wait_recv()
        gathers_b[k].start()

    def pass_c(k):
        gathers_b[k].wait_recv()
        gathers_c[k].start()

    products = []

    def consume(k):
        start, size = CHUNKS[k]
        size_wide = size + (META if k == last else 0)
        gathers_c[k].wait_recv()

        @pl.loop(0, n, unroll=4)
        def _(i):
            value = gathered[k][i // (2 * far), (i // far) % 2, i % far]
            tokens[pl.ds(2 * i, 2), :, start : start + size_wide] = value.astype(
                jnp.float32
            ).reshape(2, PIECES, size_wide)

        if k == 0:
            loads[1].wait()
            loads[2].wait()
        for j in range(PIECES):
            rows = tokens[:, j, start : start + size].astype(jnp.bfloat16)
            at = j * width + start
            products.append(
                (
                    jnp.dot(rows, wg[at : at + size, :], preferred_element_type=jnp.float32),
                    jnp.dot(rows, wu[at : at + size, :], preferred_element_type=jnp.float32),
                )
            )
            if len(products) > 1:
                later, earlier = products.pop(), products.pop()
                products.append((earlier[0] + later[0], earlier[1] + later[1]))

    def project(k):
        if k == 0:
            loads[0].wait()
            for load in loads[1:]:
                load.start()
        spread(0, k, heads, wo, None)
        if k == 0:
            pl.semaphore_wait(barrier, far + 1)
        copies_c[0][k].start()

    stages = [
        project,
        lambda k: second(0, k),
        lambda k: third(0, k),
        normed,
        pass_b,
        pass_c,
        consume,
    ]
    for step in range(len(stages) + last):
        for k in steps:
            if 0 <= step - k < len(stages):
                stages[step - k](k)

    gate, up = products[0]
    mean = (tokens[:, 0, width:] + tokens[:, 1, width:] + tokens[:, 2, width:]) * (
        1.0 / (PIECES * width)
    )
    inv_rms = lax.rsqrt(mean + EPSILON)[:, :1]
    coefs = tokens[:, 3, width:] + tokens[:, 4, width:] + tokens[:, 5, width:]
    coef = jnp.sum(jnp.where(lane == me // expert_split, coefs, 0.0), axis=1, keepdims=True)
    gate, up = gate * inv_rms, up * inv_rms
    act = (gate / (1.0 + jnp.exp(-gate)) * up).astype(jnp.bfloat16)
    loads[3].wait()

    def down(k):
        spread(1, k, act, wd, coef)
        copies_c[1][k].start()

    def final(k):
        start, size = CHUNKS[k]
        hidden[:, :, start : start + size] = hidden[:, :, start : start + size] + fourth(1, k)
        for j in range(PIECES):
            at = j * width + start
            out[:, at : at + size] = hidden[:, j, start : start + size].astype(out.dtype)

    stages = [down, lambda k: second(1, k), lambda k: third(1, k), final]
    for step in range(len(stages) + last):
        for k in steps:
            if 0 <= step - k < len(stages):
                stages[step - k](k)

    for k in steps:
        for r in range(2):
            for copy in [copies_c[r][k], copies_b[r][k]] + copies_a[r][k]:
                copy.wait_send()
        for copy in gathers_a[k] + [gathers_b[k], gathers_c[k]]:
            copy.wait_send()


def local(
    residual,
    attention,
    out_weight,
    norm_gain,
    route_ids,
    route_weight,
    gate_weight,
    up_weight,
    down_weight,
):
    n = lax.axis_size("expert")
    rows, model = residual.shape
    width = model // PIECES
    hidden_units = gate_weight.shape[2]
    far = n // 4
    count = len(CHUNKS)
    sizes = [size for _, size in CHUNKS]
    bf16, f32 = jnp.bfloat16, jnp.float32
    vmem = pl.BlockSpec(memory_space=pltpu.VMEM)
    hbm = pl.BlockSpec(memory_space=pltpu.HBM)
    dma = pltpu.SemaphoreType.DMA
    return pl.pallas_call(
        functools.partial(kernel, n, FF_WIN // hidden_units),
        out_shape=jax.ShapeDtypeStruct((rows, model), bf16),
        in_specs=[hbm] * 9,
        out_specs=vmem,
        scratch_shapes=[
            pltpu.VMEM(residual.shape, bf16),
            pltpu.VMEM(attention.shape, bf16),
            pltpu.VMEM((1, model), f32),
            pltpu.VMEM(route_ids.shape, jnp.int32),
            pltpu.VMEM(route_weight.shape, f32),
            pltpu.VMEM(out_weight.shape, bf16),
            pltpu.VMEM(gate_weight.shape[1:], bf16),
            pltpu.VMEM(up_weight.shape[1:], bf16),
            pltpu.VMEM(down_weight.shape[1:], bf16),
            [[pltpu.VMEM((2 * n, PIECES, size), f32) for size in sizes] for _ in range(2)],
            [
                pltpu.VMEM((2, 2, far, 2 * PIECES, size + META * (k == count - 1)), bf16)
                for k, size in enumerate(sizes)
            ],
            pltpu.VMEM((2 * n, PIECES, width + META), f32),
            pltpu.VMEM((2, PIECES, width), f32),
            pltpu.VMEM((PIECES, width), f32),
            pltpu.VMEM((2, PIECES, META), f32),
            [[pltpu.VMEM((n, PIECES, size), f32) for size in sizes] for _ in range(2)],
            [[pltpu.VMEM((far, 2 * PIECES, size), bf16) for size in sizes] for _ in range(2)],
            [[pltpu.VMEM((far, 2 * PIECES, size), bf16) for size in sizes] for _ in range(2)],
            [[pltpu.VMEM((far - 1, 2 * PIECES, size), bf16) for size in sizes] for _ in range(2)],
            [[pltpu.VMEM((far - 1, 2 * PIECES, size), bf16) for size in sizes] for _ in range(2)],
            dma((9,)),
            dma((2, count, 2)),
            dma((2, count, 2)),
            dma((2, count, far - 1, 2)),
            dma((count, 2)),
            dma((count, 2)),
            dma((count, far - 1, 2)),
        ],
        compiler_params=pltpu.CompilerParams(
            collective_id=0, has_side_effects=True, vmem_limit_bytes=60 * 1024 * 1024
        ),
    )(
        residual,
        attention,
        norm_gain.reshape(1, model),
        route_ids,
        route_weight,
        out_weight,
        gate_weight,
        up_weight,
        down_weight,
    )


def solution(mesh):
    return jax.shard_map(
        local,
        mesh=mesh,
        in_specs=(
            P(("groups", "expert"), None),
            P("groups", "expert"),
            P("expert", None),
            P(),
            P(("groups", "expert"), None),
            P(("groups", "expert"), None),
            P("expert", None, None),
            P("expert", None, None),
            P("expert", None, None),
        ),
        out_specs=P(("groups", "expert"), None),
        check_vma=False,
    )
```

```python
import functools

import jax
import jax.numpy as jnp
from jax import lax
from jax.experimental import pallas as pl
from jax.experimental.pallas import tpu as pltpu
from jax.sharding import PartitionSpec as P

FF_WIN = 1024
EPSILON = 1e-06
PIECES = 8
META = 128
CHUNKS = ((0, 896),)
MESH = pl.DeviceIdType.MESH


def split_three(value):
    high = value.astype(jnp.bfloat16).astype(jnp.float32)
    rest = value - high
    middle = rest.astype(jnp.bfloat16).astype(jnp.float32)
    return high, middle, rest - middle


def kernel(
    n,
    expert_split,
    residual_hbm,
    attention_hbm,
    gain_hbm,
    ids_hbm,
    weight_hbm,
    wo_hbm,
    wg_hbm,
    wu_hbm,
    wd_hbm,
    out,
    residual,
    attention,
    gain,
    route_ids,
    route_weight,
    wo,
    wg,
    wu,
    wd,
    partial,
    gathered,
    tokens,
    hidden,
    gain_tile,
    meta,
    recv_c,
    send_a,
    recv_a,
    load_sem,
    c_sem,
    a_sem,
    gc_sem,
    ga_sem,
):
    width = gain_tile.shape[1]
    top = route_ids.shape[1]
    steps = range(len(CHUNKS))
    last = len(CHUNKS) - 1
    me = lax.axis_index("expert")
    c = me % 2
    peer_c = me + 1 - 2 * c
    chips = n // 2
    peers = [lax.rem(me + 2 * d, n) for d in range(1, chips)]

    small = [
        pltpu.make_async_copy(source, target, load_sem.at[4 + place])
        for place, (source, target) in enumerate(
            [
                (attention_hbm, attention),
                (residual_hbm, residual),
                (gain_hbm, gain),
                (ids_hbm, route_ids),
                (weight_hbm, route_weight),
            ]
        )
    ]
    for load in small:
        load.start()
    loads = [
        pltpu.make_async_copy(wo_hbm, wo, load_sem.at[0]),
        pltpu.make_async_copy(wg_hbm.at[0], wg, load_sem.at[1]),
        pltpu.make_async_copy(wu_hbm.at[0], wu, load_sem.at[2]),
        pltpu.make_async_copy(wd_hbm.at[0], wd, load_sem.at[3]),
    ]
    loads[0].start()

    barrier = pltpu.get_barrier_semaphore()
    for peer in [peer_c] + peers:
        pl.semaphore_signal(barrier, inc=1, device_id={"expert": peer}, device_id_type=MESH)

    def remote(src, dst, sems, peer):
        return pltpu.make_async_remote_copy(
            src_ref=src,
            dst_ref=dst,
            send_sem=sems.at[0],
            recv_sem=sems.at[1],
            device_id={"expert": peer},
            device_id_type=MESH,
        )

    other_half, own_half = pl.ds((1 - c) * n, n), c * n
    copies_c, copies_a = [], []
    for r in range(2):
        copies_c.append([])
        copies_a.append([])
        for k in steps:
            copies_c[r].append(
                remote(partial[r][k].at[other_half], recv_c[r][k], c_sem.at[r, k], peer_c)
            )
            copies_a[r].append(
                [
                    remote(send_a[r][k].at[d], recv_a[r][k].at[d], a_sem.at[r, k, d], peers[d])
                    for d in range(chips - 1)
                ]
            )
    gathers_a, gathers_c = [], []
    for k in steps:
        own, plane = gathered[k].at[c, me // 2], gathered[k].at[c]
        gathers_a.append([remote(own, own, ga_sem.at[k, d], peers[d]) for d in range(chips - 1)])
        gathers_c.append(remote(plane, plane, gc_sem.at[k], peer_c))

    def spread(r, k, left, right, scale):
        start, size = CHUNKS[k]
        for j in range(PIECES):
            at = j * width + start
            product = jnp.dot(left, right[:, at : at + size], preferred_element_type=jnp.float32)
            partial[r][k][:, j, :] = product if scale is None else product * scale

    def pair_sum(r, k, owner):
        at = 2 * (owner // 2)
        total = partial[r][k][pl.ds(own_half + at, 2)] + recv_c[r][k][pl.ds(at, 2)]
        return total.reshape(2 * PIECES, CHUNKS[k][1])

    def second(r, k):
        copies_c[r][k].wait_recv()
        for d in range(chips - 1):
            send_a[r][k][d] = pair_sum(r, k, peers[d]).astype(jnp.bfloat16)
            copies_a[r][k][d].start()

    def third(r, k):
        total = pair_sum(r, k, me)
        for d in range(chips - 1):
            copies_a[r][k][d].wait_recv()
            total = total + recv_a[r][k][d].astype(jnp.float32)
        return total.reshape(2, PIECES, CHUNKS[k][1])

    for load in small:
        load.wait()
    place = lax.broadcasted_iota(jnp.int32, (2 * n, 2 * n), 0)
    token = lax.broadcasted_iota(jnp.int32, (2 * n, 2 * n), 1)
    bits = n.bit_length() - 1
    source = ((place & (n - 1)) >> 1) * 4 + (place >> bits) * 2 + (place & 1)
    order = jnp.where(source == token, 1.0, 0.0).astype(jnp.bfloat16)
    heads = jnp.dot(order, attention[...], preferred_element_type=jnp.float32).astype(jnp.bfloat16)
    lane = lax.broadcasted_iota(jnp.int32, (1, META), 1)
    meta[...] = jnp.zeros_like(meta)
    for row in range(2):
        coef = jnp.zeros((1, META), jnp.float32)
        for k in range(top):
            chosen = route_ids[row : row + 1, k : k + 1] == lane
            coef = coef + jnp.where(chosen, route_weight[row : row + 1, k : k + 1], 0.0)
        for place, value in enumerate(split_three(coef)):
            meta[row, 3 + place : 4 + place, :] = value
    for j in range(PIECES):
        hidden[:, j, :] = residual[:, j * width : (j + 1) * width].astype(jnp.float32)
        gain_tile[j : j + 1, :] = gain[:, j * width : (j + 1) * width]

    squares = []

    def normed(k):
        start, size = CHUNKS[k]
        value = hidden[:, :, start : start + size] + third(0, k)
        hidden[:, :, start : start + size] = value
        scaled = value * gain_tile[:, start : start + size][None]
        gathered[k][c, me // 2, :, :size] = scaled.reshape(2 * PIECES, size).astype(jnp.bfloat16)
        part = jnp.sum(jnp.sum(value * value, axis=2, keepdims=True), axis=1, keepdims=True)
        squares.append(part)
        if k == last:
            total = sum(squares[1:], squares[0])
            for row in range(2):
                spreaded = jnp.broadcast_to(total[row], (1, META))
                for place, piece in enumerate(split_three(spreaded)):
                    meta[row, place : place + 1, :] = piece
            gathered[k][c, me // 2, :, size:] = meta[...].reshape(2 * PIECES, META).astype(jnp.bfloat16)
        for copy in gathers_a[k]:
            copy.start()

    def pass_on(k):
        for copy in gathers_a[k]:
            copy.wait_recv()
        gathers_c[k].start()

    products = []

    def consume(k):
        start, size = CHUNKS[k]
        size_wide = size + (META if k == last else 0)
        gathers_c[k].wait_recv()

        @pl.loop(0, n, unroll=4)
        def _(i):
            value = gathered[k][i // chips, i % chips]
            tokens[pl.ds(2 * i, 2), :, start : start + size_wide] = value.astype(
                jnp.float32
            ).reshape(2, PIECES, size_wide)

        if k == 0:
            loads[1].wait()
            loads[2].wait()
        for j in range(PIECES):
            rows = tokens[:, j, start : start + size].astype(jnp.bfloat16)
            at = j * width + start
            products.append(
                (
                    jnp.dot(rows, wg[at : at + size, :], preferred_element_type=jnp.float32),
                    jnp.dot(rows, wu[at : at + size, :], preferred_element_type=jnp.float32),
                )
            )
            if len(products) > 1:
                later, earlier = products.pop(), products.pop()
                products.append((earlier[0] + later[0], earlier[1] + later[1]))

    def project(k):
        if k == 0:
            loads[0].wait()
            for load in loads[1:]:
                load.start()
        spread(0, k, heads, wo, None)
        if k == 0:
            pl.semaphore_wait(barrier, chips)
        copies_c[0][k].start()

    stages = [
        project,
        lambda k: second(0, k),
        normed,
        pass_on,
        consume,
    ]
    for step in range(len(stages) + last):
        for k in steps:
            if 0 <= step - k < len(stages):
                stages[step - k](k)

    gate, up = products[0]
    mean = (tokens[:, 0, width:] + tokens[:, 1, width:] + tokens[:, 2, width:]) * (
        1.0 / (PIECES * width)
    )
    inv_rms = lax.rsqrt(mean + EPSILON)[:, :1]
    coefs = tokens[:, 3, width:] + tokens[:, 4, width:] + tokens[:, 5, width:]
    coef = jnp.sum(jnp.where(lane == me // expert_split, coefs, 0.0), axis=1, keepdims=True)
    gate, up = gate * inv_rms, up * inv_rms
    act = (gate / (1.0 + jnp.exp(-gate)) * up).astype(jnp.bfloat16)
    loads[3].wait()

    def down(k):
        spread(1, k, act, wd, coef)
        copies_c[1][k].start()

    def final(k):
        start, size = CHUNKS[k]
        hidden[:, :, start : start + size] = hidden[:, :, start : start + size] + third(1, k)
        for j in range(PIECES):
            at = j * width + start
            out[:, at : at + size] = hidden[:, j, start : start + size].astype(out.dtype)

    stages = [down, lambda k: second(1, k), final]
    for step in range(len(stages) + last):
        for k in steps:
            if 0 <= step - k < len(stages):
                stages[step - k](k)

    for k in steps:
        for r in range(2):
            for copy in [copies_c[r][k]] + copies_a[r][k]:
                copy.wait_send()
        for copy in gathers_a[k] + [gathers_c[k]]:
            copy.wait_send()


def local(
    residual,
    attention,
    out_weight,
    norm_gain,
    route_ids,
    route_weight,
    gate_weight,
    up_weight,
    down_weight,
):
    n = lax.axis_size("expert")
    rows, model = residual.shape
    width = model // PIECES
    hidden_units = gate_weight.shape[2]
    chips = n // 2
    count = len(CHUNKS)
    sizes = [size for _, size in CHUNKS]
    bf16, f32 = jnp.bfloat16, jnp.float32
    vmem = pl.BlockSpec(memory_space=pltpu.VMEM)
    hbm = pl.BlockSpec(memory_space=pltpu.HBM)
    dma = pltpu.SemaphoreType.DMA
    return pl.pallas_call(
        functools.partial(kernel, n, FF_WIN // hidden_units),
        out_shape=jax.ShapeDtypeStruct((rows, model), bf16),
        in_specs=[hbm] * 9,
        out_specs=vmem,
        scratch_shapes=[
            pltpu.VMEM(residual.shape, bf16),
            pltpu.VMEM(attention.shape, bf16),
            pltpu.VMEM((1, model), f32),
            pltpu.VMEM(route_ids.shape, jnp.int32),
            pltpu.VMEM(route_weight.shape, f32),
            pltpu.VMEM(out_weight.shape, bf16),
            pltpu.VMEM(gate_weight.shape[1:], bf16),
            pltpu.VMEM(up_weight.shape[1:], bf16),
            pltpu.VMEM(down_weight.shape[1:], bf16),
            [[pltpu.VMEM((2 * n, PIECES, size), f32) for size in sizes] for _ in range(2)],
            [
                pltpu.VMEM((2, chips, 2 * PIECES, size + META * (k == count - 1)), bf16)
                for k, size in enumerate(sizes)
            ],
            pltpu.VMEM((2 * n, PIECES, width + META), f32),
            pltpu.VMEM((2, PIECES, width), f32),
            pltpu.VMEM((PIECES, width), f32),
            pltpu.VMEM((2, PIECES, META), f32),
            [[pltpu.VMEM((n, PIECES, size), f32) for size in sizes] for _ in range(2)],
            [[pltpu.VMEM((chips - 1, 2 * PIECES, size), bf16) for size in sizes] for _ in range(2)],
            [[pltpu.VMEM((chips - 1, 2 * PIECES, size), bf16) for size in sizes] for _ in range(2)],
            dma((9,)),
            dma((2, count, 2)),
            dma((2, count, chips - 1, 2)),
            dma((count, 2)),
            dma((count, chips - 1, 2)),
        ],
        compiler_params=pltpu.CompilerParams(
            collective_id=0, has_side_effects=True, vmem_limit_bytes=60 * 1024 * 1024
        ),
    )(
        residual,
        attention,
        norm_gain.reshape(1, model),
        route_ids,
        route_weight,
        out_weight,
        gate_weight,
        up_weight,
        down_weight,
    )


def solution(mesh):
    return jax.shard_map(
        local,
        mesh=mesh,
        in_specs=(
            P(("groups", "expert"), None),
            P("groups", "expert"),
            P("expert", None),
            P(),
            P(("groups", "expert"), None),
            P(("groups", "expert"), None),
            P("expert", None, None),
            P("expert", None, None),
            P("expert", None, None),
        ),
        out_specs=P(("groups", "expert"), None),
        check_vma=False,
    )
```

```python
import functools

import jax
import jax.numpy as jnp
from jax import lax
from jax.experimental import pallas as pl
from jax.experimental.pallas import tpu as pltpu
from jax.sharding import PartitionSpec as P

FF_WIN = 1024
EPSILON = 1e-06
PIECES = 8
META = 128
CHUNKS = ((0, 896),)
MESH = pl.DeviceIdType.MESH


def split_three(value):
    high = value.astype(jnp.bfloat16).astype(jnp.float32)
    rest = value - high
    middle = rest.astype(jnp.bfloat16).astype(jnp.float32)
    return high, middle, rest - middle


def kernel(
    n,
    expert_split,
    residual_hbm,
    attention_hbm,
    gain_hbm,
    ids_hbm,
    weight_hbm,
    wo_hbm,
    wg_hbm,
    wu_hbm,
    wd_hbm,
    out,
    residual,
    attention,
    gain,
    route_ids,
    route_weight,
    wo,
    wg,
    wu,
    wd,
    partial,
    gathered,
    tokens,
    hidden,
    gain_tile,
    meta,
    recv_c,
    send_a,
    recv_a,
    load_sem,
    c_sem,
    a_sem,
    gc_sem,
    ga_sem,
):
    width = gain_tile.shape[1]
    top = route_ids.shape[1]
    steps = range(len(CHUNKS))
    last = len(CHUNKS) - 1
    me = lax.axis_index("expert")
    c = me % 2
    peer_c = me + 1 - 2 * c
    chips = n // 2
    peers = [lax.rem(me + 2 * d, n) for d in range(1, chips)]

    small = [
        pltpu.make_async_copy(source, target, load_sem.at[4 + place])
        for place, (source, target) in enumerate(
            [
                (attention_hbm, attention),
                (residual_hbm, residual),
                (gain_hbm, gain),
                (ids_hbm, route_ids),
                (weight_hbm, route_weight),
            ]
        )
    ]
    for load in small:
        load.start()
    loads = [
        pltpu.make_async_copy(wo_hbm, wo, load_sem.at[0]),
        pltpu.make_async_copy(wg_hbm.at[0], wg, load_sem.at[1]),
        pltpu.make_async_copy(wu_hbm.at[0], wu, load_sem.at[2]),
        pltpu.make_async_copy(wd_hbm.at[0], wd, load_sem.at[3]),
    ]
    for load in loads:
        load.start()

    barrier = pltpu.get_barrier_semaphore()
    for peer in [peer_c] + peers:
        pl.semaphore_signal(barrier, inc=1, device_id={"expert": peer}, device_id_type=MESH)

    def remote(src, dst, sems, peer):
        return pltpu.make_async_remote_copy(
            src_ref=src,
            dst_ref=dst,
            send_sem=sems.at[0],
            recv_sem=sems.at[1],
            device_id={"expert": peer},
            device_id_type=MESH,
        )

    other_half, own_half = pl.ds((1 - c) * n, n), c * n
    copies_c, copies_a = [], []
    for r in range(2):
        copies_c.append([])
        copies_a.append([])
        for k in steps:
            copies_c[r].append(
                remote(partial[r][k].at[other_half], recv_c[r][k], c_sem.at[r, k], peer_c)
            )
            copies_a[r].append(
                [
                    remote(send_a[r][k].at[d], recv_a[r][k].at[d], a_sem.at[r, k, d], peers[d])
                    for d in range(chips - 1)
                ]
            )
    sources = [lax.rem(me // 2 + chips - d, chips) for d in range(chips)]
    gathers_a, gathers_c = [], []
    for k in steps:
        own = gathered[k].at[c, me // 2]
        gathers_a.append([remote(own, own, ga_sem.at[k, d], peers[d]) for d in range(chips - 1)])
        blocks = [gathered[k].at[c, place] for place in sources]
        gathers_c.append(
            [remote(blocks[d], blocks[d], gc_sem.at[k, d], peer_c) for d in range(chips)]
        )

    def spread(r, k, left, right, scale):
        start, size = CHUNKS[k]
        for j in range(PIECES):
            at = j * width + start
            product = jnp.dot(left, right[:, at : at + size], preferred_element_type=jnp.float32)
            partial[r][k][:, j, :] = product if scale is None else product * scale

    def pair_sum(r, k, owner):
        at = 2 * (owner // 2)
        total = partial[r][k][pl.ds(own_half + at, 2)] + recv_c[r][k][pl.ds(at, 2)]
        return total.reshape(2 * PIECES, CHUNKS[k][1])

    def second(r, k):
        copies_c[r][k].wait_recv()
        for d in range(chips - 1):
            send_a[r][k][d] = pair_sum(r, k, peers[d]).astype(jnp.bfloat16)
            copies_a[r][k][d].start()

    def third(r, k):
        total = pair_sum(r, k, me)
        for d in range(chips - 1):
            copies_a[r][k][d].wait_recv()
            total = total + recv_a[r][k][d].astype(jnp.float32)
        return total.reshape(2, PIECES, CHUNKS[k][1])

    for load in small:
        load.wait()
    place = lax.broadcasted_iota(jnp.int32, (2 * n, 2 * n), 0)
    token = lax.broadcasted_iota(jnp.int32, (2 * n, 2 * n), 1)
    bits = n.bit_length() - 1
    source = ((place & (n - 1)) >> 1) * 4 + (place >> bits) * 2 + (place & 1)
    order = jnp.where(source == token, 1.0, 0.0).astype(jnp.bfloat16)
    heads = jnp.dot(order, attention[...], preferred_element_type=jnp.float32).astype(jnp.bfloat16)
    lane = lax.broadcasted_iota(jnp.int32, (1, META), 1)
    meta[...] = jnp.zeros_like(meta)
    for row in range(2):
        coef = jnp.zeros((1, META), jnp.float32)
        for k in range(top):
            chosen = route_ids[row : row + 1, k : k + 1] == lane
            coef = coef + jnp.where(chosen, route_weight[row : row + 1, k : k + 1], 0.0)
        for place, value in enumerate(split_three(coef)):
            meta[row, 3 + place : 4 + place, :] = value
    for j in range(PIECES):
        hidden[:, j, :] = residual[:, j * width : (j + 1) * width].astype(jnp.float32)
        gain_tile[j : j + 1, :] = gain[:, j * width : (j + 1) * width]

    squares = []

    def normed(k):
        start, size = CHUNKS[k]
        value = hidden[:, :, start : start + size] + third(0, k)
        hidden[:, :, start : start + size] = value
        scaled = value * gain_tile[:, start : start + size][None]
        gathered[k][c, me // 2, :, :size] = scaled.reshape(2 * PIECES, size).astype(jnp.bfloat16)
        part = jnp.sum(jnp.sum(value * value, axis=2, keepdims=True), axis=1, keepdims=True)
        squares.append(part)
        if k == last:
            total = sum(squares[1:], squares[0])
            for row in range(2):
                spreaded = jnp.broadcast_to(total[row], (1, META))
                for place, piece in enumerate(split_three(spreaded)):
                    meta[row, place : place + 1, :] = piece
            gathered[k][c, me // 2, :, size:] = meta[...].reshape(2 * PIECES, META).astype(jnp.bfloat16)
        for copy in gathers_a[k]:
            copy.start()
        gathers_c[k][0].start()

    def pass_on(k):
        widen(k, c, sources[0])
        for d in range(1, chips):
            gathers_a[k][d - 1].wait_recv()
            gathers_c[k][d].start()
            widen(k, c, sources[d])

    def widen(k, core, place):
        start, size = CHUNKS[k]
        size_wide = size + (META if k == last else 0)
        value = gathered[k][core, place].astype(jnp.float32)
        tokens[pl.ds(2 * (core * chips + place), 2), :, start : start + size_wide] = value.reshape(
            2, PIECES, size_wide
        )

    products = []

    def consume(k):
        start, size = CHUNKS[k]
        for d in range(chips):
            gathers_c[k][d].wait_recv()
            widen(k, 1 - c, sources[d])
        if k == 0:
            loads[1].wait()
            loads[2].wait()
        for j in range(PIECES):
            rows = tokens[:, j, start : start + size].astype(jnp.bfloat16)
            at = j * width + start
            products.append(
                (
                    jnp.dot(rows, wg[at : at + size, :], preferred_element_type=jnp.float32),
                    jnp.dot(rows, wu[at : at + size, :], preferred_element_type=jnp.float32),
                )
            )
            if len(products) > 1:
                later, earlier = products.pop(), products.pop()
                products.append((earlier[0] + later[0], earlier[1] + later[1]))

    def project(k):
        if k == 0:
            loads[0].wait()
        spread(0, k, heads, wo, None)
        if k == 0:
            pl.semaphore_wait(barrier, chips)
        copies_c[0][k].start()

    stages = [
        project,
        lambda k: second(0, k),
        normed,
        pass_on,
        consume,
    ]
    for step in range(len(stages) + last):
        for k in steps:
            if 0 <= step - k < len(stages):
                stages[step - k](k)

    gate, up = products[0]
    mean = (tokens[:, 0, width:] + tokens[:, 1, width:] + tokens[:, 2, width:]) * (
        1.0 / (PIECES * width)
    )
    inv_rms = lax.rsqrt(mean + EPSILON)[:, :1]
    coefs = tokens[:, 3, width:] + tokens[:, 4, width:] + tokens[:, 5, width:]
    coef = jnp.sum(jnp.where(lane == me // expert_split, coefs, 0.0), axis=1, keepdims=True)
    gate, up = gate * inv_rms, up * inv_rms
    act = (gate / (1.0 + jnp.exp(-gate)) * up).astype(jnp.bfloat16)
    loads[3].wait()

    def down(k):
        spread(1, k, act, wd, coef)
        copies_c[1][k].start()

    def final(k):
        start, size = CHUNKS[k]
        hidden[:, :, start : start + size] = hidden[:, :, start : start + size] + third(1, k)
        for j in range(PIECES):
            at = j * width + start
            out[:, at : at + size] = hidden[:, j, start : start + size].astype(out.dtype)

    stages = [down, lambda k: second(1, k), final]
    for step in range(len(stages) + last):
        for k in steps:
            if 0 <= step - k < len(stages):
                stages[step - k](k)

    for k in steps:
        for r in range(2):
            for copy in [copies_c[r][k]] + copies_a[r][k]:
                copy.wait_send()
        for copy in gathers_a[k] + gathers_c[k]:
            copy.wait_send()


def local(
    residual,
    attention,
    out_weight,
    norm_gain,
    route_ids,
    route_weight,
    gate_weight,
    up_weight,
    down_weight,
):
    n = lax.axis_size("expert")
    rows, model = residual.shape
    width = model // PIECES
    hidden_units = gate_weight.shape[2]
    chips = n // 2
    count = len(CHUNKS)
    sizes = [size for _, size in CHUNKS]
    bf16, f32 = jnp.bfloat16, jnp.float32
    vmem = pl.BlockSpec(memory_space=pltpu.VMEM)
    hbm = pl.BlockSpec(memory_space=pltpu.HBM)
    dma = pltpu.SemaphoreType.DMA
    return pl.pallas_call(
        functools.partial(kernel, n, FF_WIN // hidden_units),
        out_shape=jax.ShapeDtypeStruct((rows, model), bf16),
        in_specs=[hbm] * 9,
        out_specs=vmem,
        scratch_shapes=[
            pltpu.VMEM(residual.shape, bf16),
            pltpu.VMEM(attention.shape, bf16),
            pltpu.VMEM((1, model), f32),
            pltpu.VMEM(route_ids.shape, jnp.int32),
            pltpu.VMEM(route_weight.shape, f32),
            pltpu.VMEM(out_weight.shape, bf16),
            pltpu.VMEM(gate_weight.shape[1:], bf16),
            pltpu.VMEM(up_weight.shape[1:], bf16),
            pltpu.VMEM(down_weight.shape[1:], bf16),
            [[pltpu.VMEM((2 * n, PIECES, size), f32) for size in sizes] for _ in range(2)],
            [
                pltpu.VMEM((2, chips, 2 * PIECES, size + META * (k == count - 1)), bf16)
                for k, size in enumerate(sizes)
            ],
            pltpu.VMEM((2 * n, PIECES, width + META), f32),
            pltpu.VMEM((2, PIECES, width), f32),
            pltpu.VMEM((PIECES, width), f32),
            pltpu.VMEM((2, PIECES, META), f32),
            [[pltpu.VMEM((n, PIECES, size), f32) for size in sizes] for _ in range(2)],
            [[pltpu.VMEM((chips - 1, 2 * PIECES, size), bf16) for size in sizes] for _ in range(2)],
            [[pltpu.VMEM((chips - 1, 2 * PIECES, size), bf16) for size in sizes] for _ in range(2)],
            dma((9,)),
            dma((2, count, 2)),
            dma((2, count, chips - 1, 2)),
            dma((count, chips, 2)),
            dma((count, chips - 1, 2)),
        ],
        compiler_params=pltpu.CompilerParams(
            collective_id=0, has_side_effects=True, vmem_limit_bytes=60 * 1024 * 1024
        ),
    )(
        residual,
        attention,
        norm_gain.reshape(1, model),
        route_ids,
        route_weight,
        out_weight,
        gate_weight,
        up_weight,
        down_weight,
    )


def solution(mesh):
    return jax.shard_map(
        local,
        mesh=mesh,
        in_specs=(
            P(("groups", "expert"), None),
            P("groups", "expert"),
            P("expert", None),
            P(),
            P(("groups", "expert"), None),
            P(("groups", "expert"), None),
            P("expert", None, None),
            P("expert", None, None),
            P("expert", None, None),
        ),
        out_specs=P(("groups", "expert"), None),
        check_vma=False,
    )
```
